32 devices in a mesh: member: 2 (over y), lon: 16 (over z, x, core).
Axes of the slice: x: 2, y: 2, z: 4, core: 2. Of those that a mesh axis runs over, the one named last changes fastest.
Arguments:
- increment: bfloat16 [137, 256, 384], P(None, ('member', 'lon')), parts along dimension 1, may hold values from -6 to 6
- kernels: float32 [5, 25], replicated, may hold values from -1.5 to 1.5
- covariance: bfloat16 [5, 16, 137, 137], replicated, may hold values from -16 to 16, as said below
- region: int32 [16, 3], replicated, may hold values from 0 to 15
Outputs:
- balanced: bfloat16 [137, 256, 384], P(None, ('member', 'lon')), parts along dimension 1
The draws below stay inside these ranges and needn't reach their ends.
There are 2 independent parts, one for each index of `member`. The reference program is written for one: setup_inputs(seed, part) draws one part's arguments, and reference() takes and returns one part's arrays. A program takes and returns all parts, laid end to end along the dimension named above; an argument that names none is the same for every part. Nothing has to cross between parts.
Inputs may be any that keep to these rules, and one draw needn't show every extreme that they name: `region`: each entry names one of the 16 regional blocks. `covariance`: each matrix is full.
All inputs are finite; a program needn't handle non-finite values.
Results may differ from the reference program's by a relative error of at most 0.0058.
Values may be sent and summed in bfloat16 or wider, within the bound.
No kernel may reach another device: no remote copies, remote signals or barrier semaphores. Data moves between devices by JAX's collectives and lax.ppermute only.
A program may use at most 128 MiB of HBM per device.

```python
import math
import jax
import jax.numpy as jnp
from jax import lax

NLEV = 137
LEVELS = 4
BANDS = 5
LON_DEV = 8
LAT = 384
NREG = 16
TILES = 16
NLON = 128
LATBLK = 3


def draw_covariance(key, part):
    noise_key, diag_key = jax.random.split(key, 2)
    noise_draw = jnp.clip(jax.random.normal(noise_key, (BANDS, NREG, NLEV, NLEV), jnp.float32), -4.0, 4.0)
    diagonal = jax.random.uniform(diag_key, (BANDS, NREG, NLEV, 1), jnp.float32, 0.6, 1.4)
    identity = jnp.eye(NLEV, dtype=jnp.float32)
    matrices = diagonal * identity + noise_draw * (0.5 / math.sqrt(NLEV))
    band_gain = jnp.exp2(0.5 * jnp.arange(BANDS, dtype=jnp.float32)).reshape(BANDS, 1, 1, 1)
    return (matrices * band_gain).astype(jnp.bfloat16)


def plant(values, stream_key, low, top_value):
    index_at = [jax.random.randint(jax.random.fold_in(stream_key, axis), (), 0, length) for axis, length in enumerate(values.shape)]
    main_axis = values.shape.index(max(values.shape))
    neighbour = index_at[:main_axis] + [(index_at[main_axis] + 1) % values.shape[main_axis]] + index_at[main_axis + 1:]
    return values.at[tuple(index_at)].set(low).at[tuple(neighbour)].set(top_value)


def steps_of(key, shape, cuts, least, top_value):
    level, own = 1.0, jax.random.fold_in(key, 6)
    for axis_at, parts in cuts:
        draws = jnp.exp(jax.random.uniform(jax.random.fold_in(own, axis_at), (parts,), jnp.float32, least / len(cuts), top_value / len(cuts)))
        level = level * jnp.repeat(draws, shape[axis_at] // parts).reshape([-1 if axis == axis_at else 1 for axis in range(len(shape))])
    return level


def centred(own_key, extent, width, limit, cuts=(), kind=jnp.bfloat16):
    factor_of = steps_of(own_key, extent, cuts, -0.22, 0.18) if cuts else 1.0
    array = jax.random.normal(own_key, extent, jnp.float32) * width * factor_of
    return jnp.minimum(jnp.maximum(array, -limit), limit).astype(kind)


def setup_inputs(seed: int = 0, part: int = 0) -> dict:
    arg_keys = jax.random.split(jax.random.key(seed), 5)
    part_splits = jax.random.split(jax.random.fold_in(arg_keys[4], part), 5)
    increment = centred(part_splits[0], (NLEV, NLON, LAT), 1.0, 6.0, ((1, 16),))
    kernels = centred(arg_keys[1], (BANDS, 25), 0.25, 1.5, (), jnp.float32)
    covariance = draw_covariance(jax.random.fold_in(arg_keys[4], 71), part)
    region = plant(jax.random.randint(arg_keys[3], (TILES, LATBLK), 0, NREG), jax.random.fold_in(arg_keys[3], 1), 0, NREG - 1).astype(jnp.int32)
    return dict(increment=increment, kernels=kernels, covariance=covariance, region=region)


def filter_padded(padded, weights):
    lon_count = padded.shape[1] - 4
    lat_count = padded.shape[2] - 4
    summed = jnp.zeros((padded.shape[0], lon_count, lat_count), jnp.float32)
    for row_shift in range(5):
        for col_shift in range(5):
            window = padded[:, row_shift:row_shift + lon_count, col_shift:col_shift + lat_count]
            summed = summed + weights[row_shift * 5 + col_shift] * window.astype(jnp.float32)
    return summed.astype(jnp.bfloat16)


def filter_band(band_field, weights):
    padded = jnp.pad(band_field, ((0, 0), (0, 0), (2, 2)))
    padded = jnp.concatenate([padded[:, -2:], padded, padded[:, :2]], axis=1)
    return filter_padded(padded, weights)


def vertical(filtered, matrices, region):
    level_count, lon_count, lat_count = filtered.shape
    tile_count, block_count = region.shape
    chosen = matrices[region].astype(jnp.float32)
    grid = filtered.astype(jnp.float32).reshape(level_count, tile_count, lon_count // tile_count, block_count, lat_count // block_count)
    result = jnp.einsum("tqab,btxqr->atxqr", chosen, grid, precision=lax.Precision.HIGHEST)
    return result.reshape(level_count, lon_count, lat_count)


def reference(increment, kernels, covariance, region):
    smooth = increment.astype(jnp.float32)
    level_count, lon_count, lat_count = smooth.shape
    summed = jnp.zeros(smooth.shape, jnp.float32)
    for tier_index in range(LEVELS):
        pair_span = (2 ** tier_index) * LON_DEV
        halves = smooth.reshape(level_count, lon_count // (2 * pair_span), 2, pair_span, lat_count)
        paired = (0.5 * (halves + halves[:, :, ::-1])).reshape(smooth.shape)
        band_field = (smooth - paired).astype(jnp.bfloat16)
        summed = summed + vertical(filter_band(band_field, kernels[tier_index]), covariance[tier_index], region)
        smooth = paired
    coarse = smooth.astype(jnp.bfloat16)
    summed = summed + vertical(filter_band(coarse, kernels[LEVELS]), covariance[LEVELS], region)
    return summed.astype(jnp.bfloat16)
```

```python
import functools

import jax
import jax.numpy as jnp
from jax import lax
from jax.experimental import pallas as pl
from jax.experimental.pallas import tpu as pltpu
from jax.sharding import PartitionSpec as P

LEVELS = 4
BANDS = 5
LANES = 128
F32 = jnp.float32
BF16 = jnp.bfloat16


def up(value, unit):
    return -(-value // unit) * unit


def swap(field, bit, count):
    return lax.ppermute(field, "lon", [(t, t ^ (1 << bit)) for t in range(count)])


def outer_swap(edge, level, count):
    route = []
    for t in range(1, count, 2):
        if (t + 1) % (2 << level) == 0:
            route += [(t, (t + 1) % count), ((t + 1) % count, t)]
    return lax.ppermute(edge, "lon", route)


def prep_kernel(taps, weights):
    row = lax.broadcasted_iota(jnp.int32, (LANES, LANES), 0)
    col = lax.broadcasted_iota(jnp.int32, (LANES, LANES), 1)
    place = (row + 2) & (LANES - 1)
    own = place >> 2
    end = place & 3
    edge_at = jnp.where(end < 2, end - 2, LANES - 2 + end)
    zero = jnp.zeros((LANES, LANES), F32)
    for k in range(BANDS):
        inside, edges = [], []
        for a in range(5):
            body, side = zero, zero
            for b in range(5):
                tap = taps[k, 5 * a + b]
                body = body + jnp.where(row - col == b - 2, tap, 0.0)
                side = side + jnp.where(edge_at - col == b - 2, tap, 0.0)
            inside.append(body.astype(BF16))
            edges.append(side)
        for u in range(6):
            for v in range(2):
                a = u - v
                block = inside[a] if 0 <= a < 5 else zero.astype(BF16)
                weights[k, u * LANES:(u + 1) * LANES, v * LANES:(v + 1) * LANES] = block
        for v in range(2):
            total = zero
            for a in range(5):
                total = total + jnp.where(own - v == a, edges[a], 0.0)
            weights[k, 6 * LANES:7 * LANES, v * LANES:(v + 1) * LANES] = total.astype(BF16)


def band_kernel(k, lons, blocks, halos, last, *refs):
    info = refs[0]
    count_r = min(k, LEVELS - 1) + 1
    refs = refs[1:]
    s0, refs = refs[0], refs[1:]
    r, refs = refs[:count_r], refs[count_r:]
    if k + 1 <= LEVELS - 1:
        r_next, refs = refs[0], refs[1:]
    else:
        r_next = None
    h, refs = dict(zip(halos, refs[:len(halos)])), refs[len(halos):]
    weights, cov, refs = refs[0], refs[1], refs[2:]
    if k > 0:
        acc_in, refs = refs[0], refs[1:]
    out, bands, ends = refs
    rows = s0.shape[1]
    pairs = lons // 2

    odd = info[0]
    far = info[1]
    outer_from = jnp.where(odd == 1, 0, lons - 2)
    inner_from = jnp.where(odd == 1, lons - 2, 0)
    outer_to = jnp.where(odd == 1, pairs + 1, 0)
    inner_to = jnp.where(odd == 1, 0, pairs + 1)

    def field(ref, at):
        return ref[pl.ds(at, 2)].astype(F32)

    def smooth(at, level):
        value = field(s0, at)
        for j in range(level):
            value = 0.5 * (value + field(r[j], at))
        return value

    def put(to, value):
        value = value.astype(BF16)
        for block in range(blocks):
            for half in range(2):
                bands[block, to, :, half * LANES:(half + 1) * LANES] = (
                    value[half, :, block * LANES:(block + 1) * LANES])

    def own(at):
        value = smooth(at, k)
        if k < LEVELS:
            value = 0.5 * (value - field(r[k], at))
        return value

    for pair in range(pairs):
        put(pair + 1, own(2 * pair))
    inner = own(inner_from)
    put(inner_to, -inner if k == 0 else inner)

    def beyond(level):
        value = smooth(outer_from, level)
        if level < LEVELS:
            partner = r[level] if level < count_r else r_next
            value = jnp.where(far == level, field(partner, outer_from), value)
        if level in h:
            first = level if level < LEVELS else level - 1
            value = jnp.where(far > first, h[level][...].astype(F32), value)
        return value

    value = beyond(k)
    if k < LEVELS:
        value = value - beyond(k + 1)
    put(outer_to, value)

    lane = lax.broadcasted_iota(jnp.int32, (rows, LANES), 1)
    none = jnp.zeros((rows, LANES), BF16)
    for block in range(blocks):
        total = none
        for n in range(lons + 4):
            at = slice((n % 2) * LANES, (n % 2 + 1) * LANES)
            after = bands[block + 1, n // 2, :, at] if block + 1 < blocks else none
            before = bands[block - 1, n // 2, :, at] if block > 0 else none
            both = jnp.where(lane < LANES // 2, after, before)
            turned = pltpu.roll(both, 4 * n, 1) if n else both
            place = (lane + 2) & (LANES - 1)
            total = jnp.where((place >> 2) == n, turned, total)
        for pair in range(pairs):
            ends[block, pair] = pltpu.roll(total, LANES - 8 * pair, 1) if pair else total

    for block in range(blocks):
        left = jnp.concatenate(
            [bands[block, 0:pairs], bands[block, 1:pairs + 1], bands[block, 2:pairs + 2], ends[block]],
            axis=2).reshape(pairs * rows, 7 * LANES)
        filtered = jnp.dot(left, weights[k], preferred_element_type=F32).astype(BF16)
        filtered = filtered.reshape(pairs, rows, 2 * LANES)
        for pair in range(pairs):
            done = jnp.dot(cov[k, block], filtered[pair], preferred_element_type=F32)
            at = slice(pair * 2 * LANES, (pair + 1) * 2 * LANES)
            if k > 0:
                done = done + acc_in[block, :, at]
            if last:
                done = done.astype(BF16)
                for half in range(2):
                    out[2 * pair + half, :, block * LANES:(block + 1) * LANES] = (
                        done[:, half * LANES:(half + 1) * LANES])
            else:
                out[block, :, at] = done


def apply_band(k, info, s0, r, h, weights, cov, acc, last):
    lons, rows, lat = s0.shape
    blocks = lat // LANES
    pairs = lons // 2
    count_r = min(k, LEVELS - 1) + 1
    halos = [level for level in (k, k + 1) if level in h]
    operands = [info, s0] + list(r[:count_r])
    if k + 1 <= LEVELS - 1:
        operands.append(r[k + 1])
    operands += [h[level] for level in halos] + [weights, cov]
    if k > 0:
        operands.append(acc)
    shape = (jax.ShapeDtypeStruct((lons, rows, lat), BF16) if last
             else jax.ShapeDtypeStruct((blocks, rows, lons * LANES), F32))
    vmem = pl.BlockSpec(memory_space=pltpu.VMEM)
    return pl.pallas_call(
        functools.partial(band_kernel, k, lons, blocks, halos, last),
        out_shape=shape,
        in_specs=[pl.BlockSpec(memory_space=pltpu.SMEM)] + [vmem] * (len(operands) - 1),
        out_specs=vmem,
        scratch_shapes=[
            pltpu.VMEM((blocks, pairs + 2, rows, 2 * LANES), BF16),
            pltpu.VMEM((blocks, pairs, rows, LANES), BF16),
        ],
        compiler_params=pltpu.CompilerParams(vmem_limit_bytes=32 << 20),
        cost_estimate=pl.CostEstimate(flops=2_000_000_000, bytes_accessed=4_000_000, transcendentals=0),
        name=f"band{k}",
    )(*operands)


def on_device(count, increment, kernels, covariance, region):
    levels, lons, lat = increment.shape
    blocks = lat // LANES
    rows = up(levels, 16)
    half, quarter = lons // 2, lons // 4
    tile = lax.axis_index("lon")
    odd = tile & 1
    second = (tile >> 1) & 1
    border = tile + odd
    far = jnp.int32(0)
    for level in range(1, count.bit_length() - 1):
        far = jnp.where(border % (1 << level) == 0, level, far)
    info = jnp.stack([odd, far]).astype(jnp.int32)
    own_region = lax.dynamic_index_in_dim(region, tile, 0, keepdims=False)

    s0 = jnp.pad(jnp.transpose(increment, (1, 0, 2)), ((0, 0), (0, rows - levels), (0, 0)))
    edge_from = odd * (lons - 2)

    r0 = swap(s0, 0, count)
    h = {0: outer_swap(lax.dynamic_slice_in_dim(s0, edge_from, 2, 0), 0, count)}

    def edge_of_half(part):
        return lax.dynamic_slice_in_dim(part, odd * (half - 2), 2, 0)

    def both(part, bit, which):
        other = swap(part, bit, count)
        low = jnp.where(which == 0, part, other)
        high = jnp.where(which == 0, other, part)
        return jnp.concatenate([low, high], 0)

    own_half = lambda x: lax.dynamic_slice_in_dim(x, odd * half, half, 0).astype(F32)
    s1 = 0.5 * (own_half(s0) + own_half(r0))
    s1_send = s1.astype(BF16)
    r1 = swap(s1_send, 1, count)
    h[1] = outer_swap(edge_of_half(s1_send), 1, count)
    s2 = 0.5 * (s1 + r1.astype(F32))
    s2_send = s2.astype(BF16)
    r2 = swap(s2_send, 2, count)
    h[2] = outer_swap(edge_of_half(s2_send), 2, count)
    s3 = 0.5 * (s2 + r2.astype(F32))
    s3_send = s3.astype(BF16)
    r3 = swap(lax.dynamic_slice_in_dim(s3_send, second * quarter, quarter, 0), 3, count)
    r1 = both(r1, 0, odd)
    r2 = both(r2, 0, odd)
    r3 = both(both(r3, 1, second), 0, odd)
    if count > 1 << LEVELS:
        h[3] = outer_swap(edge_of_half(s3_send), 3, count)
        s4 = 0.5 * (edge_of_half(s3) + edge_of_half(own_half(r3)))
        h[4] = outer_swap(s4.astype(BF16), 3, count)

    cov = jnp.stack([lax.dynamic_index_in_dim(covariance, own_region[b], 1, keepdims=False)
                     for b in range(blocks)], 1)
    cov = jnp.pad(cov, ((0, 0), (0, 0), (0, rows - levels), (0, rows - levels)))
    weights = pl.pallas_call(
        prep_kernel,
        out_shape=jax.ShapeDtypeStruct((BANDS, 7 * LANES, 2 * LANES), BF16),
        in_specs=[pl.BlockSpec(memory_space=pltpu.SMEM)],
        out_specs=pl.BlockSpec(memory_space=pltpu.VMEM),
        name="taps",
    )(kernels)

    r = [r0, r1, r2, r3]
    acc = None
    for k in range(BANDS):
        acc = apply_band(k, info, s0, r, h, weights, cov, acc, k == BANDS - 1)
    return jnp.transpose(acc[:, :levels], (1, 0, 2))


def solution(mesh):
    placed = (P(None, ("member", "lon"), None), P(), P(), P())
    return jax.shard_map(
        functools.partial(on_device, mesh.shape["lon"]),
        mesh=mesh,
        in_specs=placed,
        out_specs=P(None, ("member", "lon"), None),
        check_vma=False,
    )
```

```python
import functools

import jax
import jax.numpy as jnp
from jax import lax
from jax.experimental import pallas as pl
from jax.experimental.pallas import tpu as pltpu
from jax.sharding import PartitionSpec as P

LEVELS = 4
BANDS = 5
LANES = 128
F32 = jnp.float32
BF16 = jnp.bfloat16


def up(value, unit):
    return -(-value // unit) * unit


def swap(field, bit, count):
    return lax.ppermute(field, "lon", [(t, t ^ (1 << bit)) for t in range(count)])


def outer_swap(edge, level, count, only=False):
    route = []
    for t in range(1, count, 2):
        if (t + 1) % (2 << level) == 0 and not (only and (t + 1) % (4 << level) == 0):
            route += [(t, (t + 1) % count), ((t + 1) % count, t)]
    return lax.ppermute(edge, "lon", route)


def prep_kernel(taps, weights, masks):
    row = lax.broadcasted_iota(jnp.int32, (LANES, LANES), 0)
    col = lax.broadcasted_iota(jnp.int32, (LANES, LANES), 1)
    for b in range(5):
        masks[b] = jnp.where(row - col == b - 2, 1.0, 0.0)
    own = ((row + 2) & (LANES - 1)) >> 2
    end = (lax.broadcasted_iota(jnp.int32, (8, LANES), 0) + 2) & 3
    edge_at = jnp.where(end < 2, end - 2, LANES - 2 + end)
    reach = edge_at - lax.broadcasted_iota(jnp.int32, (8, LANES), 1)
    zero = jnp.zeros((LANES, LANES), BF16)
    for k in range(BANDS):
        inside, edges = [], []
        for a in range(5):
            body = taps[k, 5 * a] * masks[0]
            side = jnp.zeros((8, LANES), F32)
            for b in range(5):
                if b:
                    body = body + taps[k, 5 * a + b] * masks[b]
                side = jnp.where(reach == b - 2, taps[k, 5 * a + b], side)
            inside.append(body.astype(BF16))
            edges.append(jnp.concatenate([side] * (LANES // 8), 0))
        for u in range(6):
            for v in range(2):
                a = u - v
                block = inside[a] if 0 <= a < 5 else zero
                weights[k, u * LANES:(u + 1) * LANES, v * LANES:(v + 1) * LANES] = block
        for v in range(2):
            total = jnp.zeros((LANES, LANES), F32)
            for a in range(5):
                total = jnp.where(own == a + v, edges[a], total)
            weights[k, 6 * LANES:7 * LANES, v * LANES:(v + 1) * LANES] = total.astype(BF16)


def filter_bands(ks, lons, blocks, info, s0, r, h, weights, bands, ends, store):
    r, next_edge = r
    rows = s0.shape[1]
    pairs = lons // 2
    odd, far = info[0], info[1]
    outer_from = jnp.where(odd == 1, 0, lons - 2)
    inner_from = jnp.where(odd == 1, lons - 2, 0)
    outer_to = jnp.where(odd == 1, pairs + 1, 0)
    inner_to = jnp.where(odd == 1, 0, pairs + 1)

    def field(ref, at):
        return ref[pl.ds(at, 2)].astype(F32)

    def smooth(at, level):
        value = field(s0, at)
        for j in range(level):
            value = 0.5 * (value + field(r[j], at))
        return value

    def put(i, to, value):
        value = value.astype(BF16)
        for block in range(blocks):
            for half in range(2):
                bands[i, block, to, :, half * LANES:(half + 1) * LANES] = (
                    value[half, :, block * LANES:(block + 1) * LANES])

    def own(at):
        value = smooth(at, ks[0])
        got = []
        for k in ks:
            if k < LEVELS:
                partner = field(r[k], at)
                got.append(0.5 * (value - partner))
                value = 0.5 * (value + partner)
            else:
                got.append(value)
        return got

    for pair in range(pairs):
        for i, value in enumerate(own(2 * pair)):
            put(i, pair + 1, value)
    for i, value in enumerate(own(inner_from)):
        put(i, inner_to, -value if ks[i] == 0 else value)

    beyond = {}
    value = smooth(outer_from, ks[0])
    for level in range(ks[0], min(ks[-1] + 1, LEVELS) + 1):
        at_border = value
        if level < LEVELS:
            partner = field(r[level], outer_from) if level < len(r) else next_edge[...].astype(F32)
            at_border = jnp.where(far == level, partner, value)
            value = 0.5 * (value + partner)
        if level in h:
            first = level if level < LEVELS else level - 1
            at_border = jnp.where(far > first, h[level][...].astype(F32), at_border)
        beyond[level] = at_border
    for i, k in enumerate(ks):
        put(i, outer_to, beyond[k] - beyond[k + 1] if k < LEVELS else beyond[k])

    lane = lax.broadcasted_iota(jnp.int32, (rows, LANES), 1)
    place = ((lane + 2) & (LANES - 1)) >> 2
    none = jnp.zeros((rows, LANES), BF16)
    for i, k in enumerate(ks):
        for block in range(blocks):
            total = none
            for n in range(lons + 4):
                at = slice((n % 2) * LANES, (n % 2 + 1) * LANES)
                after = bands[i, block + 1, n // 2, :, at] if block + 1 < blocks else none
                before = bands[i, block - 1, n // 2, :, at] if block > 0 else none
                both = jnp.where(lane < LANES // 2, after, before)
                turned = pltpu.roll(both, 4 * n, 1) if n else both
                total = jnp.where(place == n, turned, total)
            for pair in range(pairs):
                ends[block, pair] = pltpu.roll(total, LANES - 8 * pair, 1) if pair else total
        for block in range(blocks):
            left = jnp.concatenate(
                [bands[i, block, 0:pairs], bands[i, block, 1:pairs + 1],
                 bands[i, block, 2:pairs + 2], ends[block]],
                axis=2).reshape(pairs * rows, 7 * LANES)
            filtered = jnp.dot(left, weights[k], preferred_element_type=F32).astype(BF16)
            store(i, block, filtered.reshape(pairs, rows, 2 * LANES))


def split_refs(refs, ks, halos):
    info, s0, refs = refs[0], refs[1], refs[2:]
    count_r = min(ks[-1] + 1, LEVELS)
    r, refs = refs[:count_r], refs[count_r:]
    next_edge = None
    if count_r < LEVELS:
        next_edge, refs = refs[0], refs[1:]
    h, refs = dict(zip(halos, refs[:len(halos)])), refs[len(halos):]
    return info, s0, (r, next_edge), h, refs[0], refs[1:]


def filter_kernel(ks, lons, blocks, halos, *refs):
    info, s0, r, h, weights, refs = split_refs(refs, ks, halos)
    out, bands, ends = refs

    def store(i, block, value):
        out[i, block] = value

    filter_bands(ks, lons, blocks, info, s0, r, h, weights, bands, ends, store)


def last_kernel(ks, lons, blocks, halos, *refs):
    info, s0, r, h, weights, refs = split_refs(refs, ks, halos)
    cov, acc, out, bands, ends, done = refs
    rows = s0.shape[1]
    pairs = lons // 2

    def store(i, block, value):
        done[i, block] = value

    filter_bands(ks, lons, blocks, info, s0, r, h, weights, bands, ends, store)
    for block in range(blocks):
        for pair in range(pairs):
            at = slice(pair * 2 * LANES, (pair + 1) * 2 * LANES)
            total = acc[block, :, at]
            for i, k in enumerate(ks):
                total = total + jnp.dot(cov[k, block, :, :rows], done[i, block, pair], preferred_element_type=F32)
            total = total.astype(BF16)
            for half in range(2):
                out[2 * pair + half, :, block * LANES:(block + 1) * LANES] = (
                    total[:, half * LANES:(half + 1) * LANES])


def vertical_kernel(lons, blocks, cov, *refs):
    parts, out = refs[:-1], refs[-1]
    rows = out.shape[1]
    for block in range(blocks):
        for pair in range(lons // 2):
            total, k = None, 0
            for part in parts:
                for i in range(part.shape[0]):
                    more = jnp.dot(cov[k, block, :, :rows], part[i, block, pair], preferred_element_type=F32)
                    total = more if total is None else total + more
                    k += 1
            out[block, :, pair * 2 * LANES:(pair + 1) * 2 * LANES] = total


def choose_kernel(levels, rows, blocks, place, region, every, chosen, wide, tail):
    regions = every.shape[2]
    tile = place[2]
    wide[levels * regions:, :] = jnp.zeros((wide.shape[0] - levels * regions, LANES), F32)
    tail[...] = jnp.zeros(tail.shape, F32)
    for k in range(BANDS):
        flat = every[k].astype(F32).reshape(levels * regions, levels)
        wide[:levels * regions, :] = flat[:, :LANES]
        tail[:levels * regions, :levels - LANES] = flat[:, LANES:]
        for block in range(blocks):
            at = pl.ds(region[tile, block], rows, stride=regions)
            chosen[k, block, :, :LANES] = wide[at, :].astype(BF16)
            chosen[k, block, :, LANES:] = tail[at, :].astype(BF16)


VMEM = pl.BlockSpec(memory_space=pltpu.VMEM)
SMEM = pl.BlockSpec(memory_space=pltpu.SMEM)


def cost(flops, data):
    return pl.CostEstimate(flops=int(flops), bytes_accessed=int(data), transcendentals=0)


def filter_part(ks, info, s0, r, h, weights, name, flops, cov=None, acc=None):
    lons, rows, lat = s0.shape
    blocks, pairs = lat // LANES, lons // 2
    halos = [level for level in range(ks[0], min(ks[-1] + 1, LEVELS) + 1) if level in h]
    operands = [info, s0, *r, *[h[level] for level in halos], weights]
    scratch = [pltpu.VMEM((len(ks), blocks, pairs + 2, rows, 2 * LANES), BF16),
               pltpu.VMEM((blocks, pairs, rows, LANES), BF16)]
    if cov is None:
        kernel = filter_kernel
        shape = jax.ShapeDtypeStruct((len(ks), blocks, pairs, rows, 2 * LANES), BF16)
    else:
        kernel = last_kernel
        operands += [cov, acc]
        scratch.append(pltpu.VMEM((len(ks), blocks, pairs, rows, 2 * LANES), BF16))
        shape = jax.ShapeDtypeStruct((lons, rows, lat), BF16)
    return pl.pallas_call(
        functools.partial(kernel, ks, lons, blocks, halos),
        out_shape=shape,
        in_specs=[SMEM] + [VMEM] * (len(operands) - 1),
        out_specs=VMEM,
        scratch_shapes=scratch,
        compiler_params=pltpu.CompilerParams(vmem_limit_bytes=14 << 20),
        cost_estimate=cost(flops, 1e6),
        name=name,
    )(*operands)


def on_device(count, increment, kernels, covariance, region):
    levels, lons, lat = increment.shape
    blocks = lat // LANES
    rows = up(levels, 16)
    tile = lax.axis_index("lon")
    odd = tile & 1
    second = (tile >> 1) & 1
    border = tile + odd
    far = jnp.int32(0)
    for level in range(1, count.bit_length() - 1):
        far = jnp.where(border % (1 << level) == 0, level, far)
    info = jnp.stack([odd, far, tile]).astype(jnp.int32)

    def on_rows(x):
        return jnp.pad(jnp.transpose(x, (1, 0, 2)), ((0, 0), (0, rows - levels), (0, 0)))

    def pick(which, x):
        middle = x.shape[0] // 2
        return jnp.where(which == 1, x[:middle], x[middle:])

    def pair_up(which, mine, other):
        return jnp.concatenate([jnp.where(which == 1, mine, other), jnp.where(which == 1, other, mine)], 0)

    def edge(x):
        return jnp.where(odd == 1, x[-2:], x[:2])

    def far_edge(x):
        return jnp.where(odd == 1, x[:2], x[-2:])

    def mean(a, b):
        return 0.5 * (a.astype(F32) + b.astype(F32))

    def after(x, y):
        return lax.optimization_barrier((x, y))

    def gather(x, bit, which):
        return pair_up(which, x, swap(x, bit, count))

    partner = swap(increment, 0, count)
    s0 = on_rows(increment)
    r0 = on_rows(partner)
    s1 = mean(pick(odd, s0), pick(odd, r0))
    s1_send = s1.astype(BF16)
    r1_half = swap(s1_send, 1, count)
    place, _ = after(info, s1_send)
    kernels, _ = after(kernels, s1_send)
    weights = pl.pallas_call(
        prep_kernel,
        out_shape=jax.ShapeDtypeStruct((BANDS, 7 * LANES, 2 * LANES), BF16),
        in_specs=[SMEM],
        out_specs=VMEM,
        scratch_shapes=[pltpu.VMEM((5, LANES, LANES), F32)],
        compiler_params=pltpu.CompilerParams(vmem_limit_bytes=4 << 20),
        cost_estimate=cost(1.5e9, 1e6),
        name="taps",
    )(kernels)
    regions = covariance.shape[1]
    chosen = pl.pallas_call(
        functools.partial(choose_kernel, levels, rows, blocks),
        out_shape=jax.ShapeDtypeStruct((BANDS, blocks, rows, 2 * LANES), BF16),
        in_specs=[SMEM, SMEM, VMEM],
        out_specs=VMEM,
        scratch_shapes=[pltpu.VMEM((rows * regions, LANES), F32)] * 2,
        compiler_params=pltpu.CompilerParams(vmem_limit_bytes=10 << 20),
        cost_estimate=cost(3e9, 6e6),
        name="choose",
    )(place, region, jnp.transpose(covariance, (0, 2, 1, 3)))
    sides = jnp.concatenate([edge(s0), mean(edge(s0), edge(r0)).astype(BF16)], 0)
    s2_part = mean(pick(second, s1), pick(second, r1_half))
    r2_part = swap(s2_part.astype(BF16), 2, count)
    r1 = gather(r1_half, 0, odd)
    s2_edge = mean(mean(edge(s0), edge(r0)), edge(r1)).astype(BF16)
    near = outer_swap(jnp.concatenate([sides, s2_edge], 0), 1, count)
    sides, _ = after(edge(s0), r1)
    across = outer_swap(sides, 0, count, only=True)
    middle = near[4:]
    s3_part = mean(s2_part, r2_part)
    r3_part = swap(s3_part.astype(BF16), 3, count)
    r2_half = gather(r2_part, 1, second)
    r3_part, (r2_half, across, near) = after(r3_part, (r2_half, across, near))
    r2 = gather(r2_half, 0, odd)
    middle = near[4:]
    h = {0: jnp.where(far == 1, across, near[:2]), 1: near[2:4], 2: middle}
    fine = filter_part((0, 1), info, s0, (r0, r1, r2_part), h, weights, "fine", 8e8)
    r3_half = gather(r3_part, 1, second)
    if count > 1 << LEVELS:
        s3_edge = mean(mean(mean(edge(s0), edge(r0)), edge(r1)), edge(r2))
        h[3] = outer_swap(s3_edge.astype(BF16), 3, count)
    third = filter_part((2,), info, s0, (r0, r1, r2, r3_part), h, weights, "third", 4e8)
    acc = pl.pallas_call(
        functools.partial(vertical_kernel, lons, blocks),
        out_shape=jax.ShapeDtypeStruct((blocks, rows, lons * LANES), F32),
        in_specs=[VMEM] * 3,
        out_specs=VMEM,
        compiler_params=pltpu.CompilerParams(vmem_limit_bytes=8 << 20),
        cost_estimate=cost(5e8, 1e6),
        name="vertical",
    )(chosen, fine, third)
    r3_half, acc = after(r3_half, acc)
    r3 = gather(r3_half, 0, odd)
    if count > 1 << LEVELS:
        s4_edge = mean(s3_edge, edge(r3))
        h[4] = outer_swap(s4_edge.astype(BF16), 3, count)
    out = filter_part((3, 4), info, s0, (r0, r1, r2, r3), h, weights, "last", 1e9, chosen, acc)
    return jnp.transpose(out[:, :levels], (1, 0, 2))


def solution(mesh):
    placed = (P(None, ("member", "lon"), None), P(), P(), P())
    return jax.shard_map(
        functools.partial(on_device, mesh.shape["lon"]),
        mesh=mesh,
        in_specs=placed,
        out_specs=P(None, ("member", "lon"), None),
        check_vma=False,
    )
```

```python
import functools

import jax
import jax.numpy as jnp
from jax import lax
from jax.experimental import pallas as pl
from jax.experimental.pallas import tpu as pltpu
from jax.sharding import PartitionSpec as P

LEVELS = 4
BANDS = 5
LANES = 128
F32 = jnp.float32
BF16 = jnp.bfloat16


def up(value, unit):
    return -(-value // unit) * unit


def swap(field, bit, count):
    return lax.ppermute(field, "lon", [(t, t ^ (1 << bit)) for t in range(count)])


def outer_swap(edge, level, count, only=False):
    route = []
    for t in range(1, count, 2):
        if (t + 1) % (2 << level) == 0 and not (only and (t + 1) % (4 << level) == 0):
            route += [(t, (t + 1) % count), ((t + 1) % count, t)]
    return lax.ppermute(edge, "lon", route)


def prep_kernel(taps, weights, masks):
    row = lax.broadcasted_iota(jnp.int32, (LANES, LANES), 0)
    col = lax.broadcasted_iota(jnp.int32, (LANES, LANES), 1)
    for b in range(5):
        masks[b] = jnp.where(row - col == b - 2, 1.0, 0.0)
    own = ((row + 2) & (LANES - 1)) >> 2
    end = (lax.broadcasted_iota(jnp.int32, (8, LANES), 0) + 2) & 3
    edge_at = jnp.where(end < 2, end - 2, LANES - 2 + end)
    reach = edge_at - lax.broadcasted_iota(jnp.int32, (8, LANES), 1)
    zero = jnp.zeros((LANES, LANES), BF16)
    for k in range(BANDS):
        inside, edges = [], []
        for a in range(5):
            body = taps[k, 5 * a] * masks[0]
            side = jnp.zeros((8, LANES), F32)
            for b in range(5):
                if b:
                    body = body + taps[k, 5 * a + b] * masks[b]
                side = jnp.where(reach == b - 2, taps[k, 5 * a + b], side)
            inside.append(body.astype(BF16))
            edges.append(jnp.concatenate([side] * (LANES // 8), 0))
        for u in range(6):
            for v in range(2):
                a = u - v
                block = inside[a] if 0 <= a < 5 else zero
                weights[k, u * LANES:(u + 1) * LANES, v * LANES:(v + 1) * LANES] = block
        for v in range(2):
            total = jnp.zeros((LANES, LANES), F32)
            for a in range(5):
                total = jnp.where(own == a + v, edges[a], total)
            weights[k, 6 * LANES:7 * LANES, v * LANES:(v + 1) * LANES] = total.astype(BF16)


def filter_bands(ks, lons, blocks, info, s0, r, h, weights, bands, ends, store):
    r, next_edge = r
    rows = s0.shape[1]
    pairs = lons // 2
    odd, far = info[0], info[1]
    outer_from = jnp.where(odd == 1, 0, lons - 2)
    inner_from = jnp.where(odd == 1, lons - 2, 0)
    outer_to = jnp.where(odd == 1, pairs + 1, 0)
    inner_to = jnp.where(odd == 1, 0, pairs + 1)

    def field(ref, at):
        return ref[pl.ds(at, 2)].astype(F32)

    def smooth(at, level):
        value = field(s0, at)
        for j in range(level):
            value = 0.5 * (value + field(r[j], at))
        return value

    def put(i, to, value):
        value = value.astype(BF16)
        for block in range(blocks):
            for half in range(2):
                bands[i, block, to, :, half * LANES:(half + 1) * LANES] = (
                    value[half, :, block * LANES:(block + 1) * LANES])

    def own(at):
        value = smooth(at, ks[0])
        got = []
        for k in ks:
            if k < LEVELS:
                partner = field(r[k], at)
                got.append(0.5 * (value - partner))
                value = 0.5 * (value + partner)
            else:
                got.append(value)
        return got

    for pair in range(pairs):
        for i, value in enumerate(own(2 * pair)):
            put(i, pair + 1, value)
    for i, value in enumerate(own(inner_from)):
        put(i, inner_to, -value if ks[i] == 0 else value)

    beyond = {}
    value = smooth(outer_from, ks[0])
    for level in range(ks[0], min(ks[-1] + 1, LEVELS) + 1):
        at_border = value
        if level < LEVELS:
            partner = field(r[level], outer_from) if level < len(r) else next_edge[...].astype(F32)
            at_border = jnp.where(far == level, partner, value)
            value = 0.5 * (value + partner)
        if level in h:
            first = level if level < LEVELS else level - 1
            at_border = jnp.where(far > first, h[level][...].astype(F32), at_border)
        beyond[level] = at_border
    for i, k in enumerate(ks):
        put(i, outer_to, beyond[k] - beyond[k + 1] if k < LEVELS else beyond[k])

    lane = lax.broadcasted_iota(jnp.int32, (rows, LANES), 1)
    place = ((lane + 2) & (LANES - 1)) >> 2
    none = jnp.zeros((rows, LANES), BF16)
    for i, k in enumerate(ks):
        for block in range(blocks):
            total = none
            for n in range(lons + 4):
                at = slice((n % 2) * LANES, (n % 2 + 1) * LANES)
                after = bands[i, block + 1, n // 2, :, at] if block + 1 < blocks else none
                before = bands[i, block - 1, n // 2, :, at] if block > 0 else none
                both = jnp.where(lane < LANES // 2, after, before)
                turned = pltpu.roll(both, 4 * n, 1) if n else both
                total = jnp.where(place == n, turned, total)
            for pair in range(pairs):
                ends[block, pair] = pltpu.roll(total, LANES - 8 * pair, 1) if pair else total
        for block in range(blocks):
            left = jnp.concatenate(
                [bands[i, block, 0:pairs], bands[i, block, 1:pairs + 1],
                 bands[i, block, 2:pairs + 2], ends[block]],
                axis=2).reshape(pairs * rows, 7 * LANES)
            filtered = jnp.dot(left, weights[k], preferred_element_type=F32).astype(BF16)
            store(i, block, filtered.reshape(pairs, rows, 2 * LANES))


def split_refs(refs, ks, halos):
    info, s0, refs = refs[0], refs[1], refs[2:]
    count_r = min(ks[-1] + 1, LEVELS)
    r, refs = refs[:count_r], refs[count_r:]
    next_edge = None
    if count_r < LEVELS:
        next_edge, refs = refs[0], refs[1:]
    h, refs = dict(zip(halos, refs[:len(halos)])), refs[len(halos):]
    return info, s0, (r, next_edge), h, refs[0], refs[1:]


def filter_kernel(ks, lons, blocks, halos, *refs):
    info, s0, r, h, weights, refs = split_refs(refs, ks, halos)
    out, bands, ends = refs

    def store(i, block, value):
        out[i, block] = value

    filter_bands(ks, lons, blocks, info, s0, r, h, weights, bands, ends, store)


def last_kernel(ks, lons, blocks, halos, *refs):
    info, s0, r, h, weights, refs = split_refs(refs, ks, halos)
    cov, acc, out, bands, ends, done = refs
    rows = s0.shape[1]
    pairs = lons // 2

    def store(i, block, value):
        done[i, block] = value

    filter_bands(ks, lons, blocks, info, s0, r, h, weights, bands, ends, store)
    for block in range(blocks):
        for pair in range(pairs):
            at = slice(pair * 2 * LANES, (pair + 1) * 2 * LANES)
            total = acc[block, :, at]
            for i, k in enumerate(ks):
                total = total + jnp.dot(cov[k, block, :, :rows], done[i, block, pair], preferred_element_type=F32)
            total = total.astype(BF16)
            for half in range(2):
                out[2 * pair + half, :, block * LANES:(block + 1) * LANES] = (
                    total[:, half * LANES:(half + 1) * LANES])


def vertical_kernel(lons, blocks, cov, *refs):
    parts, out = refs[:-1], refs[-1]
    rows = out.shape[1]
    for block in range(blocks):
        for pair in range(lons // 2):
            total, k = None, 0
            for part in parts:
                for i in range(part.shape[0]):
                    more = jnp.dot(cov[k, block, :, :rows], part[i, block, pair], preferred_element_type=F32)
                    total = more if total is None else total + more
                    k += 1
            out[block, :, pair * 2 * LANES:(pair + 1) * 2 * LANES] = total


def choose_kernel(levels, rows, blocks, place, region, every, chosen, wide, tail):
    regions = every.shape[2]
    tile = place[2]
    wide[levels * regions:, :] = jnp.zeros((wide.shape[0] - levels * regions, LANES), F32)
    tail[...] = jnp.zeros(tail.shape, F32)
    for k in range(BANDS):
        flat = every[k].astype(F32).reshape(levels * regions, levels)
        wide[:levels * regions, :] = flat[:, :LANES]
        tail[:levels * regions, :levels - LANES] = flat[:, LANES:]
        for block in range(blocks):
            at = pl.ds(region[tile, block], rows, stride=regions)
            chosen[k, block, :, :LANES] = wide[at, :].astype(BF16)
            chosen[k, block, :, LANES:] = tail[at, :].astype(BF16)


VMEM = pl.BlockSpec(memory_space=pltpu.VMEM)
SMEM = pl.BlockSpec(memory_space=pltpu.SMEM)


def cost(flops, data):
    return pl.CostEstimate(flops=int(flops), bytes_accessed=int(data), transcendentals=0)


def filter_part(ks, info, s0, r, h, weights, name, flops, cov=None, acc=None):
    lons, rows, lat = s0.shape
    blocks, pairs = lat // LANES, lons // 2
    halos = [level for level in range(ks[0], min(ks[-1] + 1, LEVELS) + 1) if level in h]
    operands = [info, s0, *r, *[h[level] for level in halos], weights]
    scratch = [pltpu.VMEM((len(ks), blocks, pairs + 2, rows, 2 * LANES), BF16),
               pltpu.VMEM((blocks, pairs, rows, LANES), BF16)]
    if cov is None:
        kernel = filter_kernel
        shape = jax.ShapeDtypeStruct((len(ks), blocks, pairs, rows, 2 * LANES), BF16)
    else:
        kernel = last_kernel
        operands += [cov, acc]
        scratch.append(pltpu.VMEM((len(ks), blocks, pairs, rows, 2 * LANES), BF16))
        shape = jax.ShapeDtypeStruct((lons, rows, lat), BF16)
    return pl.pallas_call(
        functools.partial(kernel, ks, lons, blocks, halos),
        out_shape=shape,
        in_specs=[SMEM] + [VMEM] * (len(operands) - 1),
        out_specs=VMEM,
        scratch_shapes=scratch,
        compiler_params=pltpu.CompilerParams(vmem_limit_bytes=14 << 20),
        cost_estimate=cost(flops, 1e6),
        name=name,
    )(*operands)


def on_device(count, increment, kernels, covariance, region):
    levels, lons, lat = increment.shape
    blocks = lat // LANES
    rows = up(levels, 16)
    tile = lax.axis_index("lon")
    odd = tile & 1
    second = (tile >> 1) & 1
    border = tile + odd
    far = jnp.int32(0)
    for level in range(1, count.bit_length() - 1):
        far = jnp.where(border % (1 << level) == 0, level, far)
    info = jnp.stack([odd, far, tile]).astype(jnp.int32)

    def on_rows(x):
        return jnp.pad(jnp.transpose(x, (1, 0, 2)), ((0, 0), (0, rows - levels), (0, 0)))

    def pick(which, x):
        middle = x.shape[0] // 2
        return jnp.where(which == 1, x[:middle], x[middle:])

    def pair_up(which, mine, other):
        return jnp.concatenate([jnp.where(which == 1, mine, other), jnp.where(which == 1, other, mine)], 0)

    def edge(x):
        return jnp.where(odd == 1, x[-2:], x[:2])

    def far_edge(x):
        return jnp.where(odd == 1, x[:2], x[-2:])

    def mean(a, b):
        return 0.5 * (a.astype(F32) + b.astype(F32))

    def after(x, y):
        return lax.optimization_barrier((x, y))

    def gather(x, bit, which):
        return pair_up(which, x, swap(x, bit, count))

    partner = swap(increment, 0, count)
    s0 = on_rows(increment)
    r0 = on_rows(partner)
    s1 = mean(pick(odd, s0), pick(odd, r0))
    s1_send = s1.astype(BF16)
    r1_half = swap(s1_send, 1, count)
    place, _ = after(info, s1_send)
    kernels, _ = after(kernels, s1_send)
    weights = pl.pallas_call(
        prep_kernel,
        out_shape=jax.ShapeDtypeStruct((BANDS, 7 * LANES, 2 * LANES), BF16),
        in_specs=[SMEM],
        out_specs=VMEM,
        scratch_shapes=[pltpu.VMEM((5, LANES, LANES), F32)],
        compiler_params=pltpu.CompilerParams(vmem_limit_bytes=4 << 20),
        cost_estimate=cost(1.5e9, 1e6),
        name="taps",
    )(kernels)
    regions = covariance.shape[1]
    chosen = pl.pallas_call(
        functools.partial(choose_kernel, levels, rows, blocks),
        out_shape=jax.ShapeDtypeStruct((BANDS, blocks, rows, 2 * LANES), BF16),
        in_specs=[SMEM, SMEM, VMEM],
        out_specs=VMEM,
        scratch_shapes=[pltpu.VMEM((rows * regions, LANES), F32)] * 2,
        compiler_params=pltpu.CompilerParams(vmem_limit_bytes=10 << 20),
        cost_estimate=cost(3e9, 6e6),
        name="choose",
    )(place, region, jnp.transpose(covariance, (0, 2, 1, 3)))
    sides = jnp.concatenate([edge(s0), mean(edge(s0), edge(r0)).astype(BF16)], 0)
    s2_part = mean(pick(second, s1), pick(second, r1_half))
    r2_part = swap(s2_part.astype(BF16), 2, count)
    sides, _ = after(sides, weights)
    near = outer_swap(sides, 1, count)
    r1 = gather(r1_half, 0, odd)
    s2_edge = mean(mean(edge(s0), edge(r0)), edge(r1)).astype(BF16)
    middle = outer_swap(s2_edge, 2, count)
    sides, _ = after(edge(s0), r1)
    across = outer_swap(sides, 0, count, only=True)
    s3_part = mean(s2_part, r2_part)
    r3_part = swap(s3_part.astype(BF16), 3, count)
    r2_half = gather(r2_part, 1, second)
    r3_part, (r2_half, across, middle) = after(r3_part, (r2_half, across, middle))
    r2 = gather(r2_half, 0, odd)
    h = {0: jnp.where(far == 1, across, near[:2]), 1: near[2:], 2: middle}
    fine = filter_part((0, 1), info, s0, (r0, r1, r2_part), h, weights, "fine", 8e8)
    r3_half = gather(r3_part, 1, second)
    if count > 1 << LEVELS:
        s3_edge = mean(mean(mean(edge(s0), edge(r0)), edge(r1)), edge(r2))
        h[3] = outer_swap(s3_edge.astype(BF16), 3, count)
    r3_half, fine = after(r3_half, fine)
    third = filter_part((2,), info, s0, (r0, r1, r2, r3_part), h, weights, "third", 4e8)
    acc = pl.pallas_call(
        functools.partial(vertical_kernel, lons, blocks),
        out_shape=jax.ShapeDtypeStruct((blocks, rows, lons * LANES), F32),
        in_specs=[VMEM] * 3,
        out_specs=VMEM,
        compiler_params=pltpu.CompilerParams(vmem_limit_bytes=8 << 20),
        cost_estimate=cost(5e8, 1e6),
        name="vertical",
    )(chosen, fine, third)
    r3 = gather(r3_half, 0, odd)
    if count > 1 << LEVELS:
        s4_edge = mean(s3_edge, edge(r3))
        h[4] = outer_swap(s4_edge.astype(BF16), 3, count)
    out = filter_part((3, 4), info, s0, (r0, r1, r2, r3), h, weights, "last", 1e9, chosen, acc)
    return jnp.transpose(out[:, :levels], (1, 0, 2))


def solution(mesh):
    placed = (P(None, ("member", "lon"), None), P(), P(), P())
    return jax.shard_map(
        functools.partial(on_device, mesh.shape["lon"]),
        mesh=mesh,
        in_specs=placed,
        out_specs=P(None, ("member", "lon"), None),
        check_vma=False,
    )
```

```python
import functools

import jax
import jax.numpy as jnp
from jax import lax
from jax.experimental import pallas as pl
from jax.experimental.pallas import tpu as pltpu
from jax.sharding import PartitionSpec as P

LEVELS = 4
BANDS = 5
LANES = 128
F32 = jnp.float32
BF16 = jnp.bfloat16


def up(value, unit):
    return -(-value // unit) * unit


def swap(field, bit, count):
    return lax.ppermute(field, "lon", [(t, t ^ (1 << bit)) for t in range(count)])


def outer_swap(edge, level, count, only=False):
    route = []
    for t in range(1, count, 2):
        if (t + 1) % (2 << level) == 0 and not (only and (t + 1) % (4 << level) == 0):
            route += [(t, (t + 1) % count), ((t + 1) % count, t)]
    return lax.ppermute(edge, "lon", route)


def prep_kernel(taps, weights, masks):
    row = lax.broadcasted_iota(jnp.int32, (LANES, LANES), 0)
    col = lax.broadcasted_iota(jnp.int32, (LANES, LANES), 1)
    for b in range(5):
        masks[b] = jnp.where(row - col == b - 2, 1.0, 0.0)
    own = ((row + 2) & (LANES - 1)) >> 2
    end = (lax.broadcasted_iota(jnp.int32, (8, LANES), 0) + 2) & 3
    edge_at = jnp.where(end < 2, end - 2, LANES - 2 + end)
    reach = edge_at - lax.broadcasted_iota(jnp.int32, (8, LANES), 1)
    zero = jnp.zeros((LANES, LANES), BF16)
    for k in range(BANDS):
        inside, edges = [], []
        for a in range(5):
            body = taps[k, 5 * a] * masks[0]
            side = jnp.zeros((8, LANES), F32)
            for b in range(5):
                if b:
                    body = body + taps[k, 5 * a + b] * masks[b]
                side = jnp.where(reach == b - 2, taps[k, 5 * a + b], side)
            inside.append(body.astype(BF16))
            edges.append(jnp.concatenate([side] * (LANES // 8), 0))
        for u in range(6):
            for v in range(2):
                a = u - v
                block = inside[a] if 0 <= a < 5 else zero
                weights[k, u * LANES:(u + 1) * LANES, v * LANES:(v + 1) * LANES] = block
        for v in range(2):
            total = jnp.zeros((LANES, LANES), F32)
            for a in range(5):
                total = jnp.where(own == a + v, edges[a], total)
            weights[k, 6 * LANES:7 * LANES, v * LANES:(v + 1) * LANES] = total.astype(BF16)


def filter_bands(ks, lons, blocks, info, s0, r, h, weights, bands, ends, store):
    r, next_edge = r
    rows = s0.shape[1]
    pairs = lons // 2
    odd, far = info[0], info[1]
    outer_from = jnp.where(odd == 1, 0, lons - 2)
    inner_from = jnp.where(odd == 1, lons - 2, 0)
    outer_to = jnp.where(odd == 1, pairs + 1, 0)
    inner_to = jnp.where(odd == 1, 0, pairs + 1)

    def field(ref, at):
        return ref[pl.ds(at, 2)].astype(F32)

    def smooth(at, level):
        value = field(s0, at)
        for j in range(level):
            value = 0.5 * (value + field(r[j], at))
        return value

    def put(i, to, value):
        value = value.astype(BF16)
        for block in range(blocks):
            for half in range(2):
                bands[i, block, to, :, half * LANES:(half + 1) * LANES] = (
                    value[half, :, block * LANES:(block + 1) * LANES])

    def own(at):
        value = smooth(at, ks[0])
        got = []
        for k in ks:
            if k < LEVELS:
                partner = field(r[k], at)
                got.append(0.5 * (value - partner))
                value = 0.5 * (value + partner)
            else:
                got.append(value)
        return got

    for pair in range(pairs):
        for i, value in enumerate(own(2 * pair)):
            put(i, pair + 1, value)
    for i, value in enumerate(own(inner_from)):
        put(i, inner_to, -value if ks[i] == 0 else value)

    beyond = {}
    value = smooth(outer_from, ks[0])
    for level in range(ks[0], min(ks[-1] + 1, LEVELS) + 1):
        at_border = value
        if level < LEVELS:
            partner = field(r[level], outer_from) if level < len(r) else next_edge[...].astype(F32)
            at_border = jnp.where(far == level, partner, value)
            value = 0.5 * (value + partner)
        if level in h:
            first = level if level < LEVELS else level - 1
            at_border = jnp.where(far > first, h[level][...].astype(F32), at_border)
        beyond[level] = at_border
    for i, k in enumerate(ks):
        put(i, outer_to, beyond[k] - beyond[k + 1] if k < LEVELS else beyond[k])

    lane = lax.broadcasted_iota(jnp.int32, (rows, LANES), 1)
    place = ((lane + 2) & (LANES - 1)) >> 2
    none = jnp.zeros((rows, LANES), BF16)
    for i, k in enumerate(ks):
        for block in range(blocks):
            total = none
            for n in range(lons + 4):
                at = slice((n % 2) * LANES, (n % 2 + 1) * LANES)
                after = bands[i, block + 1, n // 2, :, at] if block + 1 < blocks else none
                before = bands[i, block - 1, n // 2, :, at] if block > 0 else none
                both = jnp.where(lane < LANES // 2, after, before)
                turned = pltpu.roll(both, 4 * n, 1) if n else both
                total = jnp.where(place == n, turned, total)
            for pair in range(pairs):
                ends[block, pair] = pltpu.roll(total, LANES - 8 * pair, 1) if pair else total
        for block in range(blocks):
            left = jnp.concatenate(
                [bands[i, block, 0:pairs], bands[i, block, 1:pairs + 1],
                 bands[i, block, 2:pairs + 2], ends[block]],
                axis=2).reshape(pairs * rows, 7 * LANES)
            filtered = jnp.dot(left, weights[k], preferred_element_type=F32).astype(BF16)
            store(i, block, filtered.reshape(pairs, rows, 2 * LANES))


def split_refs(refs, ks, halos):
    info, s0, refs = refs[0], refs[1], refs[2:]
    count_r = min(ks[-1] + 1, LEVELS)
    r, refs = refs[:count_r], refs[count_r:]
    next_edge = None
    if count_r < LEVELS:
        next_edge, refs = refs[0], refs[1:]
    h, refs = dict(zip(halos, refs[:len(halos)])), refs[len(halos):]
    return info, s0, (r, next_edge), h, refs[0], refs[1:]


def filter_kernel(ks, lons, blocks, halos, *refs):
    info, s0, r, h, weights, refs = split_refs(refs, ks, halos)
    out, bands, ends = refs

    def store(i, block, value):
        out[i, block] = value

    filter_bands(ks, lons, blocks, info, s0, r, h, weights, bands, ends, store)


def last_kernel(ks, lons, blocks, halos, *refs):
    info, s0, r, h, weights, refs = split_refs(refs, ks, halos)
    cov, acc, out, bands, ends, done = refs
    rows = s0.shape[1]
    pairs = lons // 2

    def store(i, block, value):
        done[i, block] = value

    filter_bands(ks, lons, blocks, info, s0, r, h, weights, bands, ends, store)
    for block in range(blocks):
        for pair in range(pairs):
            at = slice(pair * 2 * LANES, (pair + 1) * 2 * LANES)
            total = acc[block, :, at]
            for i, k in enumerate(ks):
                total = total + jnp.dot(cov[k, block, :, :rows], done[i, block, pair], preferred_element_type=F32)
            total = total.astype(BF16)
            for half in range(2):
                out[2 * pair + half, :, block * LANES:(block + 1) * LANES] = (
                    total[:, half * LANES:(half + 1) * LANES])


def vertical_kernel(lons, blocks, cov, *refs):
    parts, out = refs[:-1], refs[-1]
    rows = out.shape[1]
    for block in range(blocks):
        for pair in range(lons // 2):
            total, k = None, 0
            for part in parts:
                for i in range(part.shape[0]):
                    more = jnp.dot(cov[k, block, :, :rows], part[i, block, pair], preferred_element_type=F32)
                    total = more if total is None else total + more
                    k += 1
            out[block, :, pair * 2 * LANES:(pair + 1) * 2 * LANES] = total


def choose_kernel(levels, rows, blocks, place, region, every, chosen, wide, tail):
    regions = every.shape[2]
    tile = place[2]
    wide[levels * regions:, :] = jnp.zeros((wide.shape[0] - levels * regions, LANES), F32)
    tail[...] = jnp.zeros(tail.shape, F32)
    for k in range(BANDS):
        flat = every[k].astype(F32).reshape(levels * regions, levels)
        wide[:levels * regions, :] = flat[:, :LANES]
        tail[:levels * regions, :levels - LANES] = flat[:, LANES:]
        for block in range(blocks):
            at = pl.ds(region[tile, block], rows, stride=regions)
            chosen[k, block, :, :LANES] = wide[at, :].astype(BF16)
            chosen[k, block, :, LANES:] = tail[at, :].astype(BF16)


VMEM = pl.BlockSpec(memory_space=pltpu.VMEM)
SMEM = pl.BlockSpec(memory_space=pltpu.SMEM)


def cost(flops, data):
    return pl.CostEstimate(flops=int(flops), bytes_accessed=int(data), transcendentals=0)


def filter_part(ks, info, s0, r, h, weights, name, flops, cov=None, acc=None):
    lons, rows, lat = s0.shape
    blocks, pairs = lat // LANES, lons // 2
    halos = [level for level in range(ks[0], min(ks[-1] + 1, LEVELS) + 1) if level in h]
    operands = [info, s0, *r, *[h[level] for level in halos], weights]
    scratch = [pltpu.VMEM((len(ks), blocks, pairs + 2, rows, 2 * LANES), BF16),
               pltpu.VMEM((blocks, pairs, rows, LANES), BF16)]
    if cov is None:
        kernel = filter_kernel
        shape = jax.ShapeDtypeStruct((len(ks), blocks, pairs, rows, 2 * LANES), BF16)
    else:
        kernel = last_kernel
        operands += [cov, acc]
        scratch.append(pltpu.VMEM((len(ks), blocks, pairs, rows, 2 * LANES), BF16))
        shape = jax.ShapeDtypeStruct((lons, rows, lat), BF16)
    return pl.pallas_call(
        functools.partial(kernel, ks, lons, blocks, halos),
        out_shape=shape,
        in_specs=[SMEM] + [VMEM] * (len(operands) - 1),
        out_specs=VMEM,
        scratch_shapes=scratch,
        compiler_params=pltpu.CompilerParams(vmem_limit_bytes=14 << 20),
        cost_estimate=cost(flops, 1e6),
        name=name,
    )(*operands)


def on_device(count, increment, kernels, covariance, region):
    levels, lons, lat = increment.shape
    blocks = lat // LANES
    rows = up(levels, 16)
    tile = lax.axis_index("lon")
    odd = tile & 1
    second = (tile >> 1) & 1
    border = tile + odd
    far = jnp.int32(0)
    for level in range(1, count.bit_length() - 1):
        far = jnp.where(border % (1 << level) == 0, level, far)
    info = jnp.stack([odd, far, tile]).astype(jnp.int32)

    def on_rows(x):
        return jnp.pad(jnp.transpose(x, (1, 0, 2)), ((0, 0), (0, rows - levels), (0, 0)))

    def pick(which, x):
        middle = x.shape[0] // 2
        return jnp.where(which == 1, x[:middle], x[middle:])

    def pair_up(which, mine, other):
        return jnp.concatenate([jnp.where(which == 1, mine, other), jnp.where(which == 1, other, mine)], 0)

    def edge(x):
        return jnp.where(odd == 1, x[-2:], x[:2])

    def far_edge(x):
        return jnp.where(odd == 1, x[:2], x[-2:])

    def mean(a, b):
        return 0.5 * (a.astype(F32) + b.astype(F32))

    def after(x, y):
        return lax.optimization_barrier((x, y))

    def gather(x, bit, which):
        return pair_up(which, x, swap(x, bit, count))

    partner = swap(increment, 0, count)
    s0 = on_rows(increment)
    r0 = on_rows(partner)
    s1 = mean(pick(odd, s0), pick(odd, r0))
    s1_send = s1.astype(BF16)
    r1_half = swap(s1_send, 1, count)
    place, _ = after(info, s1_send)
    kernels, _ = after(kernels, s1_send)
    weights = pl.pallas_call(
        prep_kernel,
        out_shape=jax.ShapeDtypeStruct((BANDS, 7 * LANES, 2 * LANES), BF16),
        in_specs=[SMEM],
        out_specs=VMEM,
        scratch_shapes=[pltpu.VMEM((5, LANES, LANES), F32)],
        compiler_params=pltpu.CompilerParams(vmem_limit_bytes=4 << 20),
        cost_estimate=cost(1.5e9, 1e6),
        name="taps",
    )(kernels)
    regions = covariance.shape[1]
    chosen = pl.pallas_call(
        functools.partial(choose_kernel, levels, rows, blocks),
        out_shape=jax.ShapeDtypeStruct((BANDS, blocks, rows, 2 * LANES), BF16),
        in_specs=[SMEM, SMEM, VMEM],
        out_specs=VMEM,
        scratch_shapes=[pltpu.VMEM((rows * regions, LANES), F32)] * 2,
        compiler_params=pltpu.CompilerParams(vmem_limit_bytes=10 << 20),
        cost_estimate=cost(3e9, 6e6),
        name="choose",
    )(place, region, jnp.transpose(covariance, (0, 2, 1, 3)))
    sides = jnp.concatenate([edge(s0), mean(edge(s0), edge(r0)).astype(BF16)], 0)
    s2_part = mean(pick(second, s1), pick(second, r1_half))
    s2_part, (chosen, weights) = after(s2_part, (chosen, weights))
    r2_part = swap(s2_part.astype(BF16), 2, count)
    sides, _ = after(sides, weights)
    near = outer_swap(sides, 1, count)
    r1 = gather(r1_half, 0, odd)
    s2_edge = mean(mean(edge(s0), edge(r0)), edge(r1)).astype(BF16)
    middle = outer_swap(s2_edge, 2, count)
    sides, _ = after(edge(s0), r1)
    across = outer_swap(sides, 0, count, only=True)
    s3_part = mean(s2_part, r2_part)
    r3_part = swap(s3_part.astype(BF16), 3, count)
    r2_half = gather(r2_part, 1, second)
    r3_part, (r2_half, across, middle) = after(r3_part, (r2_half, across, middle))
    r2 = gather(r2_half, 0, odd)
    h = {0: jnp.where(far == 1, across, near[:2]), 1: near[2:], 2: middle}
    fine = filter_part((0, 1), info, s0, (r0, r1, r2_part), h, weights, "fine", 8e8)
    r3_half = gather(r3_part, 1, second)
    if count > 1 << LEVELS:
        s3_edge = mean(mean(mean(edge(s0), edge(r0)), edge(r1)), edge(r2))
        h[3] = outer_swap(s3_edge.astype(BF16), 3, count)
    third = filter_part((2,), info, s0, (r0, r1, r2, r3_part), h, weights, "third", 4e8)
    r3_half, (fine, third) = after(r3_half, (fine, third))
    acc = pl.pallas_call(
        functools.partial(vertical_kernel, lons, blocks),
        out_shape=jax.ShapeDtypeStruct((blocks, rows, lons * LANES), F32),
        in_specs=[VMEM] * 3,
        out_specs=VMEM,
        compiler_params=pltpu.CompilerParams(vmem_limit_bytes=8 << 20),
        cost_estimate=cost(5e8, 1e6),
        name="vertical",
    )(chosen, fine, third)
    r3 = gather(r3_half, 0, odd)
    if count > 1 << LEVELS:
        s4_edge = mean(s3_edge, edge(r3))
        h[4] = outer_swap(s4_edge.astype(BF16), 3, count)
    out = filter_part((3, 4), info, s0, (r0, r1, r2, r3), h, weights, "last", 1e9, chosen, acc)
    return jnp.transpose(out[:, :levels], (1, 0, 2))


def solution(mesh):
    placed = (P(None, ("member", "lon"), None), P(), P(), P())
    return jax.shard_map(
        functools.partial(on_device, mesh.shape["lon"]),
        mesh=mesh,
        in_specs=placed,
        out_specs=P(None, ("member", "lon"), None),
        check_vma=False,
    )
```

```python
import functools

import jax
import jax.numpy as jnp
from jax import lax
from jax.experimental import pallas as pl
from jax.experimental.pallas import tpu as pltpu
from jax.sharding import PartitionSpec as P

LEVELS = 4
BANDS = 5
LANES = 128
F32 = jnp.float32
BF16 = jnp.bfloat16


def up(value, unit):
    return -(-value // unit) * unit


def swap(field, bit, count):
    return lax.ppermute(field, "lon", [(t, t ^ (1 << bit)) for t in range(count)])


def outer_swap(edge, level, count, only=False):
    route = []
    for t in range(1, count, 2):
        if (t + 1) % (2 << level) == 0 and not (only and (t + 1) % (4 << level) == 0):
            route += [(t, (t + 1) % count), ((t + 1) % count, t)]
    return lax.ppermute(edge, "lon", route)


def prep_kernel(taps, weights, masks):
    row = lax.broadcasted_iota(jnp.int32, (LANES, LANES), 0)
    col = lax.broadcasted_iota(jnp.int32, (LANES, LANES), 1)
    for b in range(5):
        masks[b] = jnp.where(row - col == b - 2, 1.0, 0.0)
    own = ((row + 2) & (LANES - 1)) >> 2
    end = (lax.broadcasted_iota(jnp.int32, (8, LANES), 0) + 2) & 3
    edge_at = jnp.where(end < 2, end - 2, LANES - 2 + end)
    reach = edge_at - lax.broadcasted_iota(jnp.int32, (8, LANES), 1)
    zero = jnp.zeros((LANES, LANES), BF16)
    for k in range(BANDS):
        inside, edges = [], []
        for a in range(5):
            body = taps[k, 5 * a] * masks[0]
            side = jnp.zeros((8, LANES), F32)
            for b in range(5):
                if b:
                    body = body + taps[k, 5 * a + b] * masks[b]
                side = jnp.where(reach == b - 2, taps[k, 5 * a + b], side)
            inside.append(body.astype(BF16))
            edges.append(jnp.concatenate([side] * (LANES // 8), 0))
        for u in range(6):
            for v in range(2):
                a = u - v
                block = inside[a] if 0 <= a < 5 else zero
                weights[k, u * LANES:(u + 1) * LANES, v * LANES:(v + 1) * LANES] = block
        for v in range(2):
            total = jnp.zeros((LANES, LANES), F32)
            for a in range(5):
                total = jnp.where(own == a + v, edges[a], total)
            weights[k, 6 * LANES:7 * LANES, v * LANES:(v + 1) * LANES] = total.astype(BF16)


def filter_bands(ks, lons, blocks, info, s0, r, h, weights, bands, ends, store):
    r, next_edge = r
    rows = s0.shape[1]
    pairs = lons // 2
    odd, far = info[0], info[1]
    outer_from = jnp.where(odd == 1, 0, lons - 2)
    inner_from = jnp.where(odd == 1, lons - 2, 0)
    outer_to = jnp.where(odd == 1, pairs + 1, 0)
    inner_to = jnp.where(odd == 1, 0, pairs + 1)

    def field(ref, at):
        return ref[pl.ds(at, 2)].astype(F32)

    def smooth(at, level):
        value = field(s0, at)
        for j in range(level):
            value = 0.5 * (value + field(r[j], at))
        return value

    def put(i, to, value):
        value = value.astype(BF16)
        for block in range(blocks):
            for half in range(2):
                bands[i, block, to, :, half * LANES:(half + 1) * LANES] = (
                    value[half, :, block * LANES:(block + 1) * LANES])

    def own(at):
        value = smooth(at, ks[0])
        got = []
        for k in ks:
            if k < LEVELS:
                partner = field(r[k], at)
                got.append(0.5 * (value - partner))
                value = 0.5 * (value + partner)
            else:
                got.append(value)
        return got

    for pair in range(pairs):
        for i, value in enumerate(own(2 * pair)):
            put(i, pair + 1, value)
    for i, value in enumerate(own(inner_from)):
        put(i, inner_to, -value if ks[i] == 0 else value)

    beyond = {}
    value = smooth(outer_from, ks[0])
    for level in range(ks[0], min(ks[-1] + 1, LEVELS) + 1):
        at_border = value
        if level < LEVELS:
            partner = field(r[level], outer_from) if level < len(r) else next_edge[...].astype(F32)
            at_border = jnp.where(far == level, partner, value)
            value = 0.5 * (value + partner)
        if level in h:
            first = level if level < LEVELS else level - 1
            at_border = jnp.where(far > first, h[level][...].astype(F32), at_border)
        beyond[level] = at_border
    for i, k in enumerate(ks):
        put(i, outer_to, beyond[k] - beyond[k + 1] if k < LEVELS else beyond[k])

    lane = lax.broadcasted_iota(jnp.int32, (rows, LANES), 1)
    place = ((lane + 2) & (LANES - 1)) >> 2
    none = jnp.zeros((rows, LANES), BF16)
    for i, k in enumerate(ks):
        for block in range(blocks):
            total = none
            for n in range(lons + 4):
                at = slice((n % 2) * LANES, (n % 2 + 1) * LANES)
                after = bands[i, block + 1, n // 2, :, at] if block + 1 < blocks else none
                before = bands[i, block - 1, n // 2, :, at] if block > 0 else none
                both = jnp.where(lane < LANES // 2, after, before)
                turned = pltpu.roll(both, 4 * n, 1) if n else both
                total = jnp.where(place == n, turned, total)
            for pair in range(pairs):
                ends[block, pair] = pltpu.roll(total, LANES - 8 * pair, 1) if pair else total
        for block in range(blocks):
            left = jnp.concatenate(
                [bands[i, block, 0:pairs], bands[i, block, 1:pairs + 1],
                 bands[i, block, 2:pairs + 2], ends[block]],
                axis=2).reshape(pairs * rows, 7 * LANES)
            filtered = jnp.dot(left, weights[k], preferred_element_type=F32).astype(BF16)
            store(i, block, filtered.reshape(pairs, rows, 2 * LANES))


def split_refs(refs, ks, halos):
    info, s0, refs = refs[0], refs[1], refs[2:]
    count_r = min(ks[-1] + 1, LEVELS)
    r, refs = refs[:count_r], refs[count_r:]
    next_edge = None
    if count_r < LEVELS:
        next_edge, refs = refs[0], refs[1:]
    h, refs = dict(zip(halos, refs[:len(halos)])), refs[len(halos):]
    return info, s0, (r, next_edge), h, refs[0], refs[1:]


def filter_kernel(ks, lons, blocks, halos, *refs):
    info, s0, r, h, weights, refs = split_refs(refs, ks, halos)
    out, bands, ends = refs

    def store(i, block, value):
        out[i, block] = value

    filter_bands(ks, lons, blocks, info, s0, r, h, weights, bands, ends, store)


def last_kernel(ks, lons, blocks, halos, *refs):
    info, s0, r, h, weights, refs = split_refs(refs, ks, halos)
    cov, acc, out, bands, ends, done, turned = refs
    levels = out.shape[0]
    rows = s0.shape[1]
    pairs = lons // 2

    def store(i, block, value):
        done[i, block] = value

    filter_bands(ks, lons, blocks, info, s0, r, h, weights, bands, ends, store)
    for block in range(blocks):
        for pair in range(pairs):
            at = slice(pair * 2 * LANES, (pair + 1) * 2 * LANES)
            total = acc[block, :, at]
            for i, k in enumerate(ks):
                total = total + jnp.dot(cov[k, block, :, :rows], done[i, block, pair], preferred_element_type=F32)
            for half in range(2):
                turned[block, pl.ds(2 * pair + half, rows, stride=lons), :] = (
                    total[:, half * LANES:(half + 1) * LANES])
        out[:, :, block * LANES:(block + 1) * LANES] = (
            turned[block].reshape(rows, lons, LANES)[:levels].astype(BF16))


def vertical_kernel(lons, blocks, cov, *refs):
    parts, out = refs[:-1], refs[-1]
    rows = out.shape[1]
    for block in range(blocks):
        for pair in range(lons // 2):
            total, k = None, 0
            for part in parts:
                for i in range(part.shape[0]):
                    more = jnp.dot(cov[k, block, :, :rows], part[i, block, pair], preferred_element_type=F32)
                    total = more if total is None else total + more
                    k += 1
            out[block, :, pair * 2 * LANES:(pair + 1) * 2 * LANES] = total


def choose_kernel(levels, rows, blocks, place, region, every, chosen, wide, tail):
    regions = every.shape[2]
    tile = place[2]
    wide[levels * regions:, :] = jnp.zeros((wide.shape[0] - levels * regions, LANES), F32)
    tail[...] = jnp.zeros(tail.shape, F32)
    for k in range(BANDS):
        flat = every[k].astype(F32).reshape(levels * regions, levels)
        wide[:levels * regions, :] = flat[:, :LANES]
        tail[:levels * regions, :levels - LANES] = flat[:, LANES:]
        for block in range(blocks):
            at = pl.ds(region[tile, block], rows, stride=regions)
            chosen[k, block, :, :LANES] = wide[at, :].astype(BF16)
            chosen[k, block, :, LANES:] = tail[at, :].astype(BF16)


VMEM = pl.BlockSpec(memory_space=pltpu.VMEM)
SMEM = pl.BlockSpec(memory_space=pltpu.SMEM)


def cost(flops, data):
    return pl.CostEstimate(flops=int(flops), bytes_accessed=int(data), transcendentals=0)


def filter_part(ks, info, s0, r, h, weights, name, flops, cov=None, acc=None, levels=None):
    lons, rows, lat = s0.shape
    blocks, pairs = lat // LANES, lons // 2
    halos = [level for level in range(ks[0], min(ks[-1] + 1, LEVELS) + 1) if level in h]
    operands = [info, s0, *r, *[h[level] for level in halos], weights]
    scratch = [pltpu.VMEM((len(ks), blocks, pairs + 2, rows, 2 * LANES), BF16),
               pltpu.VMEM((blocks, pairs, rows, LANES), BF16)]
    if cov is None:
        kernel = filter_kernel
        shape = jax.ShapeDtypeStruct((len(ks), blocks, pairs, rows, 2 * LANES), BF16)
    else:
        kernel = last_kernel
        operands += [cov, acc]
        scratch.append(pltpu.VMEM((len(ks), blocks, pairs, rows, 2 * LANES), BF16))
        scratch.append(pltpu.VMEM((blocks, rows * lons, LANES), F32))
        shape = jax.ShapeDtypeStruct((levels, lons, lat), BF16)
    return pl.pallas_call(
        functools.partial(kernel, ks, lons, blocks, halos),
        out_shape=shape,
        in_specs=[SMEM] + [VMEM] * (len(operands) - 1),
        out_specs=VMEM,
        scratch_shapes=scratch,
        compiler_params=pltpu.CompilerParams(vmem_limit_bytes=14 << 20),
        cost_estimate=cost(flops, 1e6),
        name=name,
    )(*operands)


def on_device(count, increment, kernels, covariance, region):
    levels, lons, lat = increment.shape
    blocks = lat // LANES
    rows = up(levels, 16)
    tile = lax.axis_index("lon")
    odd = tile & 1
    second = (tile >> 1) & 1
    border = tile + odd
    far = jnp.int32(0)
    for level in range(1, count.bit_length() - 1):
        far = jnp.where(border % (1 << level) == 0, level, far)
    info = jnp.stack([odd, far, tile]).astype(jnp.int32)

    def on_rows(x):
        return jnp.pad(jnp.transpose(x, (1, 0, 2)), ((0, 0), (0, rows - levels), (0, 0)))

    def pick(which, x):
        middle = x.shape[0] // 2
        return jnp.where(which == 1, x[:middle], x[middle:])

    def pair_up(which, mine, other):
        return jnp.concatenate([jnp.where(which == 1, mine, other), jnp.where(which == 1, other, mine)], 0)

    def edge(x):
        return jnp.where(odd == 1, x[-2:], x[:2])

    def far_edge(x):
        return jnp.where(odd == 1, x[:2], x[-2:])

    def mean(a, b):
        return 0.5 * (a.astype(F32) + b.astype(F32))

    def after(x, y):
        return lax.optimization_barrier((x, y))

    def gather(x, bit, which):
        return pair_up(which, x, swap(x, bit, count))

    partner = swap(increment, 0, count)
    s0 = on_rows(increment)
    r0 = on_rows(partner)
    s1 = mean(pick(odd, s0), pick(odd, r0))
    s1_send = s1.astype(BF16)
    r1_half = swap(s1_send, 1, count)
    place, _ = after(info, s1_send)
    kernels, _ = after(kernels, s1_send)
    weights = pl.pallas_call(
        prep_kernel,
        out_shape=jax.ShapeDtypeStruct((BANDS, 7 * LANES, 2 * LANES), BF16),
        in_specs=[SMEM],
        out_specs=VMEM,
        scratch_shapes=[pltpu.VMEM((5, LANES, LANES), F32)],
        compiler_params=pltpu.CompilerParams(vmem_limit_bytes=4 << 20),
        cost_estimate=cost(1.5e9, 1e6),
        name="taps",
    )(kernels)
    regions = covariance.shape[1]
    chosen = pl.pallas_call(
        functools.partial(choose_kernel, levels, rows, blocks),
        out_shape=jax.ShapeDtypeStruct((BANDS, blocks, rows, 2 * LANES), BF16),
        in_specs=[SMEM, SMEM, VMEM],
        out_specs=VMEM,
        scratch_shapes=[pltpu.VMEM((rows * regions, LANES), F32)] * 2,
        compiler_params=pltpu.CompilerParams(vmem_limit_bytes=10 << 20),
        cost_estimate=cost(3e9, 6e6),
        name="choose",
    )(place, region, jnp.transpose(covariance, (0, 2, 1, 3)))
    sides = jnp.concatenate([edge(s0), mean(edge(s0), edge(r0)).astype(BF16)], 0)
    s2_part = mean(pick(second, s1), pick(second, r1_half))
    s2_part, (chosen, weights) = after(s2_part, (chosen, weights))
    r2_part = swap(s2_part.astype(BF16), 2, count)
    sides, _ = after(sides, weights)
    near = outer_swap(sides, 1, count)
    r1 = gather(r1_half, 0, odd)
    s2_edge = mean(mean(edge(s0), edge(r0)), edge(r1)).astype(BF16)
    middle = outer_swap(s2_edge, 2, count)
    sides, _ = after(edge(s0), r1)
    across = outer_swap(sides, 0, count, only=True)
    s3_part = mean(s2_part, r2_part)
    r3_part = swap(s3_part.astype(BF16), 3, count)
    r2_half = gather(r2_part, 1, second)
    r3_part, (r2_half, across, middle) = after(r3_part, (r2_half, across, middle))
    r2 = gather(r2_half, 0, odd)
    h = {0: jnp.where(far == 1, across, near[:2]), 1: near[2:], 2: middle}
    fine = filter_part((0, 1), info, s0, (r0, r1, r2_part), h, weights, "fine", 8e8)
    r3_half = gather(r3_part, 1, second)
    if count > 1 << LEVELS:
        s3_edge = mean(mean(mean(edge(s0), edge(r0)), edge(r1)), edge(r2))
        h[3] = outer_swap(s3_edge.astype(BF16), 3, count)
    third = filter_part((2,), info, s0, (r0, r1, r2, r3_part), h, weights, "third", 4e8)
    r3_half, (fine, third) = after(r3_half, (fine, third))
    acc = pl.pallas_call(
        functools.partial(vertical_kernel, lons, blocks),
        out_shape=jax.ShapeDtypeStruct((blocks, rows, lons * LANES), F32),
        in_specs=[VMEM] * 3,
        out_specs=VMEM,
        compiler_params=pltpu.CompilerParams(vmem_limit_bytes=8 << 20),
        cost_estimate=cost(5e8, 1e6),
        name="vertical",
    )(chosen, fine, third)
    r3 = gather(r3_half, 0, odd)
    if count > 1 << LEVELS:
        s4_edge = mean(s3_edge, edge(r3))
        h[4] = outer_swap(s4_edge.astype(BF16), 3, count)
    out = filter_part((3, 4), info, s0, (r0, r1, r2, r3), h, weights, "last", 1e9, chosen, acc, levels)
    return out


def solution(mesh):
    placed = (P(None, ("member", "lon"), None), P(), P(), P())
    return jax.shard_map(
        functools.partial(on_device, mesh.shape["lon"]),
        mesh=mesh,
        in_specs=placed,
        out_specs=P(None, ("member", "lon"), None),
        check_vma=False,
    )
```
